32 devices in a mesh: xy: 8 (over y, x, core), gz: 4 (over z).
Axes of the slice: x: 2, y: 2, z: 4, core: 2. Of those that a mesh axis runs over, the one named last changes fastest.
Arguments:
- density: float32 [1024, 2048], P('xy', 'gz'), may hold values from 0 to 1
- cotangent: float32 [6, 16, 128, 256], P(None, 'gz', 'xy'), may hold values from -6 to 6
- slope: int32 [16], P('gz'), may hold values from 0 to 4
- layer_block: int32 [16], P('gz'), may hold values from 0 to 3
- block_eps: float32 [4, 2], replicated, may hold values from 1.5 to 12
Outputs:
- grad_filtered: float32 [1024, 2048], P('xy', 'gz')
- grad_density: float32 [1024, 2048], P('xy', 'gz')
The draws below stay inside these ranges and needn't reach their ends.
All inputs are finite; a program needn't handle non-finite values.
Results may differ from the reference program's by a relative error of at most 0.0003.
Values sent between devices are 32-bit elements; how exact they have to be, the bound alone decides.
A program may use at most 64 MiB of HBM per device.

```python
import math
import jax
import jax.numpy as jnp
from jax import lax

SUB = 8
RADIUS = 32
MATS = 4
SLOPES = 5
NX = 128
NY = 256
LAYERS = 16
NXD = 1024
NYD = 2048


def touch_ends(drawn, stream_key, low, largest):
    place = [jax.random.randint(jax.random.fold_in(stream_key, axis), (), 0, length) for axis, length in enumerate(drawn.shape)]
    main_axis = drawn.shape.index(max(drawn.shape))
    neighbour = place[:main_axis] + [(place[main_axis] + 1) % drawn.shape[main_axis]] + place[main_axis + 1:]
    return drawn.at[tuple(place)].set(low).at[tuple(neighbour)].set(largest)


def block_scale(rng, extent, shards, least, largest):
    def one(axis_at, shards_of):
        draws = jax.random.uniform(jax.random.fold_in(jax.random.fold_in(rng, 6), axis_at), (shards_of,), jnp.float32, least / len(shards), largest / len(shards))
        return jnp.repeat(jnp.exp(draws), extent[axis_at] // shards_of).reshape((-1,) + (1,) * (len(extent) - axis_at - 1))

    factor_of = one(*shards[0])
    for cut in shards[1:]:
        factor_of = factor_of * one(*cut)
    return factor_of


def scatter_about(stream_key, shape, spread, most, pieces=(), kind=jnp.bfloat16):
    factor_of = block_scale(stream_key, shape, pieces, -0.22, 0.18) if pieces else 1.0
    array = jax.random.normal(stream_key, shape, jnp.float32) * spread * factor_of
    return jnp.minimum(jnp.maximum(array, -most), most).astype(kind)


def setup_inputs(seed: int = 0) -> dict:
    seeds = jax.random.split(jax.random.key(seed), 6)
    return {
        "density": jnp.clip(1.0 * jax.random.uniform(seeds[0], (NXD, NYD), jnp.float32) ** block_scale(seeds[0], (NXD, NYD), ((0, 8), (1, 4)), -0.2, 0.2), 0.0, 1.0),
        "cotangent": scatter_about(seeds[1], (6, LAYERS, NX, NY), 1.0, 6.0, ((1, 4), (2, 8)), jnp.float32),
        "slope": touch_ends(jax.random.randint(seeds[2], (LAYERS,), 0, SLOPES), jax.random.fold_in(seeds[2], 1), 0, SLOPES - 1).astype(jnp.int32),
        "layer_block": touch_ends(jax.random.randint(seeds[3], (LAYERS,), 0, MATS), jax.random.fold_in(seeds[3], 1), 0, MATS - 1).astype(jnp.int32),
        "block_eps": jnp.clip(jnp.exp(jax.random.uniform(seeds[4], (MATS, 2), jnp.float32, math.log(1.5), math.log(12.0))), 1.5, 12.0),
    }


def smooth(field):
    taps = jnp.arange(2 * RADIUS + 1)
    weights = (RADIUS + 1 - jnp.abs(taps - RADIUS)).astype(jnp.float32) / float((RADIUS + 1) ** 2)
    padded = jnp.pad(field, ((0, 0), (RADIUS, RADIUS)))
    width = field.shape[1]
    across = jnp.zeros_like(field)
    for k in range(2 * RADIUS + 1):
        across = across + weights[k] * padded[:, k:k + width]
    padded = jnp.pad(across, ((RADIUS, RADIUS), (0, 0)))
    height = field.shape[0]
    result = jnp.zeros_like(field)
    for k in range(2 * RADIUS + 1):
        result = result + weights[k] * padded[k:k + height, :]
    return result

def cell_tensor(filtered, params):
    eta, lift, eps_one, eps_two = (params[0], params[1], params[2], params[3])
    fill = jax.nn.sigmoid(32.0 * (filtered - eta))
    blocks = fill.reshape(NX, SUB, NY, SUB)
    offsets = (2.0 * jnp.arange(SUB).astype(jnp.float32) + 1.0 - SUB) / 2.0
    frac = lax.optimization_barrier(jnp.mean(blocks, axis=(1, 3)))
    grad_x = lax.optimization_barrier(jnp.mean(blocks * offsets[None, :, None, None], axis=(1, 3)))
    grad_y = lax.optimization_barrier(jnp.mean(blocks * offsets[None, None, None, :], axis=(1, 3)))
    normsq = grad_x * grad_x + grad_y * grad_y + lift * lift
    mean_eps = eps_two + frac * (eps_one - eps_two)
    mean_inv = 1.0 / eps_two + frac * (1.0 / eps_one - 1.0 / eps_two)
    weight = (1.0 / mean_inv - mean_eps) / normsq
    lifted = lift * jnp.ones_like(grad_x)
    return jnp.stack([mean_eps + weight * grad_x * grad_x, mean_eps + weight * grad_y * grad_y, mean_eps + weight * lifted * lifted, weight * grad_x * grad_y, weight * grad_x * lifted, weight * grad_y * lifted])

def reference(density, cotangent, slope, layer_block, block_eps):
    filtered = smooth(density)
    level = slope.astype(jnp.float32)
    onehot = (layer_block[:, None] == jnp.arange(MATS)[None, :]).astype(jnp.float32)
    pairs = jnp.dot(onehot, block_eps, precision=lax.Precision.HIGHEST)
    table = jnp.stack([0.5 + 0.02 * (level - 2.0), 0.2 * (1.0 + level), pairs[:, 0], pairs[:, 1]])

    def step(total, index):
        params = table[:, index]
        pullback = jax.vjp(lambda field: cell_tensor(field, params), filtered)[1]
        return (total + pullback(cotangent[:, index])[0], None)
    grad_filtered, unused = lax.scan(step, jnp.zeros_like(filtered), jnp.arange(LAYERS))
    return (grad_filtered, smooth(grad_filtered))
```

```python
import functools

import jax
import jax.numpy as jnp
from jax import lax
from jax.experimental import pallas as pl
from jax.experimental.pallas import tpu as pltpu
from jax.sharding import PartitionSpec as P

SUB = 8
RADIUS = 32
LANES = 128
BAND_COLS = 256
STEEP = 32.0
MESH = pl.DeviceIdType.MESH
F32 = jnp.float32
BF16 = jnp.bfloat16
NEAR = [(dx, dz) for dx in (-1, 0, 1) for dz in (-1, 0, 1) if (dx, dz) != (0, 0)]


def split(value, terms):
    parts = []
    for _ in range(terms):
        part = value.astype(BF16)
        parts.append(part)
        value = value - part.astype(F32)
    return parts


def iota(shape, dim):
    return lax.broadcasted_iota(jnp.int32, shape, dim)


def taps(offset):
    return jnp.maximum(RADIUS + 1 - jnp.abs(offset), 0).astype(F32).astype(BF16)


def col_band():
    shape = (BAND_COLS + 2 * LANES, BAND_COLS)
    return taps(iota(shape, 0) - LANES - iota(shape, 1))


def row_band(height):
    shape = (height, height + 2 * RADIUS)
    return taps(iota(shape, 1) - RADIUS - iota(shape, 0))


def pool_values(cell, place, other):
    offset = (2 * (place % SUB) + 1 - SUB).astype(F32) / 2.0
    inside = place // SUB == cell % other
    values = jnp.where(cell < other, 1.0, offset) / float(SUB)
    return jnp.where(inside, values, 0.0).astype(BF16)


def col_pool(width):
    shape = (width, 2 * width // SUB)
    return pool_values(iota(shape, 1), iota(shape, 0), width // SUB)


def col_pool_t(width):
    shape = (2 * width // SUB, width)
    return pool_values(iota(shape, 0), iota(shape, 1), width // SUB)


def row_pool(height):
    shape = (2 * height // SUB, height)
    return pool_values(iota(shape, 0), iota(shape, 1), height // SUB)


def row_pool_t(height):
    shape = (height, 2 * height // SUB)
    return pool_values(iota(shape, 1), iota(shape, 0), height // SUB)


def dot(a, b):
    return jnp.dot(a, b, preferred_element_type=F32)


def smooth(pad, height, width, terms):
    matrix = col_band()
    rows = row_band(height)
    scale = 1.0 / float((RADIUS + 1) ** 4)
    out = []
    for start in range(0, width, BAND_COLS):
        part = pad[:, start : start + BAND_COLS + 2 * LANES]
        across = sum(dot(x, matrix) for x in split(part, terms))
        total = sum(dot(rows, x) for x in split(across, terms))
        out.append(total * scale)
    return out


def kernel(nx, nz, rows, cols, local, slope, block, eps, density, cot, grad_out, dens_out,
           pad, gpad, stage, recv, par_send, par_recv, filt, soft, hi, lo, pooled,
           halo_send, halo_recv, grad_send, grad_recv, cot_send, cot_recv, pars_send, pars_recv):
    x = lax.axis_index("xy")
    z = lax.axis_index("gz")
    cells_x, cells_y = rows // SUB, cols // SUB
    tall, wide = rows + 2 * RADIUS, cols + 2 * LANES
    mid_r, mid_c = pl.ds(RADIUS, rows), pl.ds(LANES, cols)

    def exists(dx, dz):
        ok = None
        for pos, delta, count in ((x, dx, nx), (z, dz, nz)):
            if delta == -1:
                here = pos > 0
            elif delta == 1:
                here = pos < count - 1
            else:
                continue
            ok = here if ok is None else jnp.logical_and(ok, here)
        return ok

    for ref in (pad, gpad):
        ref[0:RADIUS, :] = jnp.zeros((RADIUS, wide), F32)
        ref[RADIUS + rows : tall, :] = jnp.zeros((RADIUS, wide), F32)
        ref[RADIUS : RADIUS + rows, 0:LANES] = jnp.zeros((rows, LANES), F32)
        ref[RADIUS : RADIUS + rows, LANES + cols : wide] = jnp.zeros((rows, LANES), F32)

    barrier = pltpu.get_barrier_semaphore()
    far = [(dx, dz) for dx, dz in NEAR if dx != 0]
    for k in range(1, nz):
        pl.semaphore_signal(barrier, inc=1, device_id=(x, lax.rem(z + k, nz)), device_id_type=MESH)
    for dx, dz in far:
        @pl.when(exists(dx, dz))
        def _():
            pl.semaphore_signal(barrier, inc=1, device_id=(x + dx, z + dz), device_id_type=MESH)

    half = iota((1, LANES), 1) < cells_y
    level = [slope[l].astype(F32) for l in range(local)]
    lines = [jnp.full((1, LANES), 0.5 + 0.02 * (v - 2.0), F32) for v in level]
    for k in range(local // 2):
        a, b = 2 * k, 2 * k + 1
        lines.append(jnp.where(half, 0.2 * (1.0 + level[a]), 0.2 * (1.0 + level[b])))
        for j in range(2):
            lines.append(jnp.where(half, eps[block[a], j], eps[block[b], j]))
    for i, line in enumerate(lines):
        par_send[i : i + 1, :] = line
    par_send[len(lines) :, :] = jnp.zeros((par_send.shape[0] - len(lines), LANES), F32)

    pl.semaphore_wait(barrier, nz - 1 + sum(jnp.where(exists(dx, dz), 1, 0) for dx, dz in far))

    def halo(source, base_r, base_c, target, send, receive, d):
        dx, dz = NEAR[d]
        src_r = {-1: pl.ds(base_r, RADIUS), 0: pl.ds(base_r, rows), 1: pl.ds(base_r + rows - RADIUS, RADIUS)}[dx]
        dst_r = {-1: pl.ds(RADIUS + rows, RADIUS), 0: mid_r, 1: pl.ds(0, RADIUS)}[dx]
        src_c = {-1: pl.ds(base_c, LANES), 0: pl.ds(base_c, cols), 1: pl.ds(base_c + cols - LANES, LANES)}[dz]
        dst_c = {-1: pl.ds(LANES + cols, LANES), 0: mid_c, 1: pl.ds(0, LANES)}[dz]
        return pltpu.make_async_remote_copy(
            src_ref=source.at[src_r, src_c], dst_ref=target.at[dst_r, dst_c],
            send_sem=send.at[d], recv_sem=receive.at[d],
            device_id=(x + dx, z + dz), device_id_type=MESH)

    def halo_each(args, what):
        for d, (dx, dz) in enumerate(NEAR):
            copy = halo(*args, d)
            where = exists(-dx, -dz) if what == "wait_recv" else exists(dx, dz)
            pl.when(where)(getattr(copy, what))

    first = (density, 0, 0, pad, halo_send, halo_recv)
    second = (gpad, RADIUS, LANES, gpad, grad_send, grad_recv)
    halo_each(first, "start")

    def peer_copy(src, dst, send, receive, k, outgoing):
        peer = lax.rem(z + k, nz)
        slot = z if outgoing else peer
        return pltpu.make_async_remote_copy(
            src_ref=src(peer), dst_ref=dst.at[slot], send_sem=send.at[k], recv_sem=receive.at[slot],
            device_id=(x, peer), device_id_type=MESH)

    def par_copy(k, outgoing):
        return peer_copy(lambda p: par_send, par_recv, pars_send, pars_recv, k, outgoing)

    def cot_copy(k, outgoing):
        return peer_copy(lambda p: stage.at[p], recv, cot_send, cot_recv, k, outgoing)

    for k in range(1, nz):
        par_copy(k, True).start()

    for c in range(cot.shape[0]):
        for k in range(local // 2):
            for h in range(nz // 2):
                a = cot[c, 2 * k, :, h * LANES : (h + 1) * LANES]
                b = cot[c, 2 * k + 1, :, h * LANES : (h + 1) * LANES]
                stage[2 * h, c, k] = jnp.where(half, a, pltpu.roll(b, cells_y, 1))
                stage[2 * h + 1, c, k] = jnp.where(half, pltpu.roll(a, cells_y, 1), b)
    for k in range(1, nz):
        cot_copy(k, True).start()
    par_recv[z] = par_send[...]
    recv[z] = stage[z]

    pad[RADIUS : RADIUS + rows, LANES : LANES + cols] = density[...]
    halo_each(first, "wait_recv")
    for i, part in enumerate(smooth(pad, rows, cols, 3)):
        filt[:, i * BAND_COLS : (i + 1) * BAND_COLS] = part
    for k in range(1, nz):
        par_copy(k, False).wait_recv()

    pool_c = col_pool(cols)
    chunk = 16

    @pl.loop(0, nz)
    def _(g):
        for l in range(local):
            eta = par_recv[g, l : l + 1, :]
            eta = jnp.concatenate([eta] * (cols // LANES), axis=1)

            @pl.loop(0, rows // chunk)
            def _(i):
                at = pl.multiple_of(i * chunk, chunk)
                fill = 1.0 / (1.0 + jnp.exp(STEEP * (eta - filt[pl.ds(at, chunk), :])))
                to = pl.ds(pl.multiple_of(at + l * rows, chunk), chunk)
                soft[g, to, :] = fill * (1.0 - fill)
                upper, lower = split(fill, 2)
                hi[to, :] = upper
                lo[to, :] = lower
        pooled[g] = dot(hi[...], pool_c) + dot(lo[...], pool_c)

    pool_r = row_pool(rows)
    pool_r2 = jnp.concatenate([pool_r, pool_r], axis=1)
    back_r = row_pool_t(rows)
    back_r2 = jnp.concatenate([back_r, back_r], axis=1)
    back_c = col_pool_t(cols)
    for k in range(1, nz):
        cot_copy(k, False).wait_recv()

    gpad[RADIUS : RADIUS + rows, LANES : LANES + cols] = jnp.zeros((rows, cols), F32)

    @pl.loop(0, nz)
    def _(g):
        zs = []
        for k in range(local // 2):
            moments = []
            for l in (2 * k, 2 * k + 1):
                upper, lower = split(pooled[g, l * rows : (l + 1) * rows, :], 2)
                moments.append(dot(pool_r2, jnp.concatenate([upper, lower], axis=0)))
            swap = lambda v: pltpu.roll(v, cells_y, 1)
            top_a, low_a = moments[0][:cells_x], moments[0][cells_x:]
            top_b, low_b = moments[1][:cells_x], moments[1][cells_x:]
            frac = jnp.where(half, top_a, swap(top_b))
            gy = jnp.where(half, swap(top_a), top_b)
            gx = jnp.where(half, low_a, swap(low_b))
            base = local + 3 * k
            cz = par_recv[g, base : base + 1, :]
            e1 = par_recv[g, base + 1 : base + 2, :]
            e2 = par_recv[g, base + 2 : base + 3, :]
            cxx, cyy, czz, cxy, cxz, cyz = (recv[g, c, k] for c in range(6))
            step = e1 - e2
            inv2 = 1.0 / e2
            inv_step = 1.0 / e1 - inv2
            norm = 1.0 / (gx * gx + gy * gy + cz * cz)
            mean = e2 + frac * step
            harm = 1.0 / (inv2 + frac * inv_step)
            weight = (harm - mean) * norm
            px = cxx * gx + cxy * gy + cxz * cz
            py = cyy * gy + cyz * cz
            quad = (gx * px + gy * py + cz * cz * czz) * norm
            d_frac = (cxx + cyy + czz - quad) * step - quad * harm * harm * inv_step
            d_gx = weight * (px + (cxx - 2.0 * quad) * gx)
            d_gy = weight * (py + (cyy - 2.0 * quad) * gy + cxy * gx)
            zero = jnp.zeros_like(d_gx)
            zs += [jnp.where(half, d_frac, swap(d_gy)), jnp.where(half, d_gx, zero),
                   jnp.where(half, swap(d_frac), d_gy), jnp.where(half, swap(d_gx), zero)]
        upper, lower = split(jnp.concatenate(zs, axis=0), 2)
        spread = dot(upper, back_c) + dot(lower, back_c)
        deep = 2 * cells_x
        for l in range(local):
            upper, lower = split(spread[l * deep : (l + 1) * deep], 2)
            pixels = dot(back_r2, jnp.concatenate([upper, lower], axis=0))
            gpad[RADIUS : RADIUS + rows, LANES : LANES + cols] += pixels * soft[g, l * rows : (l + 1) * rows, :]

    own = gpad[RADIUS : RADIUS + rows, LANES : LANES + cols] * STEEP
    gpad[RADIUS : RADIUS + rows, LANES : LANES + cols] = own
    halo_each(second, "start")
    grad_out[...] = own
    halo_each(second, "wait_recv")
    for i, part in enumerate(smooth(gpad, rows, cols, 2)):
        dens_out[:, i * BAND_COLS : (i + 1) * BAND_COLS] = part

    halo_each(first, "wait_send")
    halo_each(second, "wait_send")
    for k in range(1, nz):
        par_copy(k, True).wait_send()
        cot_copy(k, True).wait_send()


def on_device(density, cot, slope, layer_block, block_eps, nx, nz):
    rows, cols = density.shape
    comps, local = cot.shape[:2]
    cells_x = rows // SUB
    tall, wide = rows + 2 * RADIUS, cols + 2 * LANES
    packed = (nz, comps, local // 2, cells_x, LANES)
    vmem = pl.BlockSpec(memory_space=pltpu.VMEM)
    smem = pl.BlockSpec(memory_space=pltpu.SMEM)
    dma = pltpu.SemaphoreType.DMA
    near = len(NEAR)
    shape = jax.ShapeDtypeStruct((rows, cols), F32)
    return pl.pallas_call(
        functools.partial(kernel, nx, nz, rows, cols, local),
        out_shape=(shape, shape),
        in_specs=[smem, smem, smem, vmem, vmem],
        out_specs=(vmem, vmem),
        scratch_shapes=[
            pltpu.VMEM((tall, wide), F32),
            pltpu.VMEM((tall, wide), F32),
            pltpu.VMEM(packed, F32),
            pltpu.VMEM(packed, F32),
            pltpu.VMEM((16, LANES), F32),
            pltpu.VMEM((nz, 16, LANES), F32),
            pltpu.VMEM((rows, cols), F32),
            pltpu.VMEM((nz, local * rows, cols), F32),
            pltpu.VMEM((local * rows, cols), BF16),
            pltpu.VMEM((local * rows, cols), BF16),
            pltpu.VMEM((nz, local * rows, LANES), F32),
            dma((near,)), dma((near,)), dma((near,)), dma((near,)),
            dma((nz,)), dma((nz,)), dma((nz,)), dma((nz,)),
        ],
        compiler_params=pltpu.CompilerParams(
            collective_id=0, has_side_effects=True, vmem_limit_bytes=40 * 1024 * 1024),
    )(slope, layer_block, block_eps, density, cot)


def solution(mesh):
    body = functools.partial(on_device, nx=mesh.shape["xy"], nz=mesh.shape["gz"])
    return jax.shard_map(
        body,
        mesh=mesh,
        in_specs=(P("xy", "gz"), P(None, "gz", "xy", None), P("gz"), P("gz"), P()),
        out_specs=(P("xy", "gz"), P("xy", "gz")),
        check_vma=False,
    )
```

```python
import functools
import math

import jax
import jax.numpy as jnp
from jax import lax
from jax.experimental import pallas as pl
from jax.experimental.pallas import tpu as pltpu
from jax.sharding import PartitionSpec as P

SUB = 8
RADIUS = 32
SLOPES = 5
LANES = 128
BAND_COLS = 256
STEEP = 32.0
MESH = pl.DeviceIdType.MESH
F32 = jnp.float32
BF16 = jnp.bfloat16
NEAR = [(dx, dz) for dx in (-1, 0, 1) for dz in (-1, 0, 1) if (dx, dz) != (0, 0)]


def split(value, terms):
    parts = []
    for _ in range(terms):
        part = value.astype(BF16)
        parts.append(part)
        value = value - part.astype(F32)
    return parts


def iota(shape, dim):
    return lax.broadcasted_iota(jnp.int32, shape, dim)


def taps(offset):
    return jnp.maximum(RADIUS + 1 - jnp.abs(offset), 0).astype(F32).astype(BF16)


def col_band():
    shape = (BAND_COLS + 2 * LANES, BAND_COLS)
    return taps(iota(shape, 0) - LANES - iota(shape, 1))


def row_band(height):
    shape = (height, height + 2 * RADIUS)
    return taps(iota(shape, 1) - RADIUS - iota(shape, 0))


def pool_values(cell, place, other):
    offset = (2 * (place % SUB) + 1 - SUB).astype(F32) / 2.0
    inside = place // SUB == cell % other
    values = jnp.where(cell < other, 1.0, offset) / float(SUB)
    return jnp.where(inside, values, 0.0).astype(BF16)


def col_pool(width):
    shape = (width, 2 * width // SUB)
    return pool_values(iota(shape, 1), iota(shape, 0), width // SUB)


def col_pool_t(width):
    shape = (2 * width // SUB, width)
    return pool_values(iota(shape, 0), iota(shape, 1), width // SUB)


def row_pool(height):
    shape = (2 * height // SUB, height)
    return pool_values(iota(shape, 0), iota(shape, 1), height // SUB)


def row_pool_t(height):
    shape = (height, 2 * height // SUB)
    return pool_values(iota(shape, 1), iota(shape, 0), height // SUB)


def dot(a, b):
    return jnp.dot(a, b, preferred_element_type=F32)


def smooth(pad, band_c, band_r, height, width, terms):
    scale = 1.0 / float((RADIUS + 1) ** 4)
    out = []
    for start in range(0, width, BAND_COLS):
        part = pad[:, start : start + BAND_COLS + 2 * LANES]
        across = sum(dot(x, band_c[...]) for x in split(part, terms))
        total = sum(dot(band_r[...], x) for x in split(across, terms))
        out.append(total * scale)
    return out


def pack_cols(block):
    groups = LANES // RADIUS
    height = block.shape[0] // groups
    lane = iota((1, LANES), 1)
    out = block[:height]
    for j in range(1, groups):
        moved = pltpu.roll(block[j * height : (j + 1) * height], j * RADIUS, 1)
        out = jnp.where(lane >= j * RADIUS, moved, out)
    return out


def kernel(nx, nz, rows, cols, local, slope, block, eps_hbm, density_hbm, cot_hbm, grad_out, dens_out,
           pad, gpad, strip_out, strip_in, cot, eps, stage, recv, power, soft, result,
           band_c, band_r, pool_c, back_c, pool_r2, back_r2,
           in_sem, out_sem, halo_send, halo_recv, cot_send, cot_recv):
    x = lax.axis_index("xy")
    z = lax.axis_index("gz")
    cells_x, cells_y = rows // SUB, cols // SUB
    tall, wide = rows + 2 * RADIUS, cols + 2 * LANES
    mid_r, mid_c = pl.ds(RADIUS, rows), pl.ds(LANES, cols)
    groups = LANES // RADIUS

    fetch_density = pltpu.make_async_copy(density_hbm, pad.at[mid_r, mid_c], in_sem.at[0])
    fetch_cot = pltpu.make_async_copy(cot_hbm, cot, in_sem.at[1])
    fetch_eps = pltpu.make_async_copy(eps_hbm, eps, in_sem.at[2])
    fetch_density.start()
    fetch_eps.start()
    fetch_cot.start()

    def exists(dx, dz):
        ok = None
        for pos, delta, count in ((x, dx, nx), (z, dz, nz)):
            if delta == -1:
                here = pos > 0
            elif delta == 1:
                here = pos < count - 1
            else:
                continue
            ok = here if ok is None else jnp.logical_and(ok, here)
        return ok

    for ref in (pad, gpad):
        ref[0:RADIUS, mid_c] = jnp.zeros((RADIUS, cols), F32)
        ref[RADIUS + rows : tall, mid_c] = jnp.zeros((RADIUS, cols), F32)
    strip_in[...] = jnp.zeros(strip_in.shape, F32)

    barrier = pltpu.get_barrier_semaphore()
    far = [(dx, dz) for dx, dz in NEAR if dx != 0]
    for k in range(1, nz):
        pl.semaphore_signal(barrier, inc=1, device_id=(x, lax.rem(z + k, nz)), device_id_type=MESH)
    for dx, dz in far:
        @pl.when(exists(dx, dz))
        def _():
            pl.semaphore_signal(barrier, inc=1, device_id=(x + dx, z + dz), device_id_type=MESH)

    quarter, corner = rows // groups, RADIUS // groups
    spots = {0: (0, quarter), -1: (quarter, corner), 1: (quarter + corner, corner)}

    def pack_strips(source, phase):
        for side, start in ((0, 0), (1, cols - LANES)):
            edge = source[RADIUS : RADIUS + rows, LANES + start : 2 * LANES + start]
            if side == 1:
                edge = pltpu.roll(edge, RADIUS, 1)
            strip_out[phase, side, 0:quarter] = pack_cols(edge)
            strip_out[phase, side, quarter : quarter + corner] = pack_cols(edge[:RADIUS])
            strip_out[phase, side, quarter + corner :] = pack_cols(edge[rows - RADIUS :])

    def unpack_strips(target, phase):
        for side, column, shift in ((0, 0, LANES - RADIUS), (1, LANES + cols, 0)):
            for first, height, at in ((0, quarter, RADIUS), (quarter, corner, RADIUS + rows), (quarter + corner, corner, 0)):
                packed = strip_in[phase, side, first : first + height]
                for j in range(groups):
                    turn = (shift - j * RADIUS) % LANES
                    moved = pltpu.roll(packed, turn, 1) if turn else packed
                    target[at + j * height : at + (j + 1) * height, column : column + LANES] = moved

    def halo(target, phase, d):
        dx, dz = NEAR[d]
        if dz == 0:
            src = target.at[pl.ds(RADIUS if dx < 0 else rows, RADIUS), mid_c]
            dst = target.at[pl.ds(RADIUS + rows if dx < 0 else 0, RADIUS), mid_c]
        else:
            at = pl.ds(*spots[dx])
            src = strip_out.at[phase, 0 if dz < 0 else 1, at]
            dst = strip_in.at[phase, 1 if dz < 0 else 0, at]
        return pltpu.make_async_remote_copy(
            src_ref=src, dst_ref=dst, send_sem=halo_send.at[phase, d], recv_sem=halo_recv.at[phase, d],
            device_id=(x + dx, z + dz), device_id_type=MESH)

    def halo_each(target, phase, what, flat=(True, False)):
        for d, (dx, dz) in enumerate(NEAR):
            if (dz == 0) in flat:
                copy = halo(target, phase, d)
                where = exists(-dx, -dz) if what == "wait_recv" else exists(dx, dz)
                pl.when(where)(getattr(copy, what))

    fetch_density.wait()
    pack_strips(pad, 0)
    band_c[...] = col_band()
    band_r[...] = row_band(rows)
    pl.semaphore_wait(barrier, nz - 1 + sum(jnp.where(exists(dx, dz), 1, 0) for dx, dz in far))
    halo_each(pad, 0, "start")

    half = iota((1, LANES), 1) < cells_y
    swap = lambda v: pltpu.roll(v, cells_y, 1)
    comps = cot.shape[0]
    fetch_eps.wait()
    lines = []
    for k in range(local // 2):
        a, b = 2 * k, 2 * k + 1
        lines.append(jnp.where(half, slope[a].astype(F32), slope[b].astype(F32)))
        pair = jnp.where(half, block[a], block[b])
        for j in range(2):
            line = jnp.zeros((1, LANES), F32)
            for m in range(eps.shape[1]):
                line = jnp.where(pair == m, eps[j : j + 1, m : m + 1], line)
            lines.append(line)
    lines.append(jnp.zeros((cells_x - len(lines), LANES), F32))
    lines = jnp.concatenate(lines, axis=0)
    fetch_cot.wait()
    for c in range(comps):
        for k in range(local // 2):
            for h in range(nz // 2):
                a = cot[c, 2 * k, :, h * LANES : (h + 1) * LANES]
                b = cot[c, 2 * k + 1, :, h * LANES : (h + 1) * LANES]
                stage[2 * h, c * (local // 2) + k] = jnp.where(half, a, swap(b))
                stage[2 * h + 1, c * (local // 2) + k] = jnp.where(half, swap(a), b)
    for g in range(nz):
        stage[g, comps * (local // 2)] = lines

    def cot_copy(k, outgoing):
        peer = lax.rem(z + k, nz)
        slot = z if outgoing else peer
        return pltpu.make_async_remote_copy(
            src_ref=stage.at[peer], dst_ref=recv.at[slot], send_sem=cot_send.at[k], recv_sem=cot_recv.at[slot],
            device_id=(x, peer), device_id_type=MESH)

    for k in range(1, nz):
        cot_copy(k, True).start()

    pool_c[...] = col_pool(cols)
    back_c[...] = col_pool_t(cols)
    pool_r = row_pool(rows)
    pool_r2[...] = jnp.concatenate([pool_r, pool_r], axis=1)
    back_r = row_pool_t(rows)
    back_r2[...] = jnp.concatenate([back_r, back_r], axis=1)

    halo_each(pad, 0, "wait_recv")
    unpack_strips(pad, 0)
    for i, part in enumerate(smooth(pad, band_c, band_r, rows, cols, 3)):
        power[:, i * BAND_COLS : (i + 1) * BAND_COLS] = jnp.exp(STEEP * (0.5 - part))

    moments = []
    for c in range(SLOPES):
        fill = 1.0 / (1.0 + power[...] * math.exp(STEEP * 0.02 * (c - 2)))
        soft[c] = fill * (1.0 - fill)
        upper, lower = split(fill, 2)
        pooled = dot(upper, pool_c[...]) + dot(lower, pool_c[...])
        cell = dot(pool_r2[...], jnp.concatenate(split(pooled, 2), axis=0))
        top, low = cell[:cells_x], cell[cells_x:]
        turned = swap(top)
        moments.append((jnp.where(half, top, turned), jnp.where(half, low, swap(low)), jnp.where(half, turned, top)))

    totals = [[jnp.zeros((cells_x, LANES), F32)] * 3 for _ in range(SLOPES)]
    for g in range(nz):
        slot = lax.rem(z + g, nz)
        if g:
            cot_copy(g, False).wait_recv()
        held = recv if g else stage
        for k in range(local // 2):
            at = comps * (local // 2)
            kind, e1, e2 = (held[slot, at, 3 * k + j : 3 * k + j + 1, :] for j in range(3))
            cxx, cyy, czz, cxy, cxz, cyz = (held[slot, c * (local // 2) + k] for c in range(comps))
            masks = [jnp.broadcast_to(kind == float(c), (cells_x, LANES)) for c in range(SLOPES)]
            frac, gx, gy = moments[0]
            for c in range(1, SLOPES):
                frac, gx, gy = (jnp.where(masks[c], new, old) for new, old in zip(moments[c], (frac, gx, gy)))
            cz = 0.2 * (1.0 + kind)
            step = e1 - e2
            inv2 = 1.0 / e2
            inv_step = 1.0 / e1 - inv2
            norm = 1.0 / (gx * gx + gy * gy + cz * cz)
            mean = e2 + frac * step
            harm = 1.0 / (inv2 + frac * inv_step)
            weight = (harm - mean) * norm
            px = cxx * gx + cxy * gy + cxz * cz
            py = cyy * gy + cyz * cz
            quad = (gx * px + gy * py + cz * cz * czz) * norm
            adjoint = ((cxx + cyy + czz - quad) * step - quad * harm * harm * inv_step,
                       weight * (px + (cxx - 2.0 * quad) * gx),
                       weight * (py + (cyy - 2.0 * quad) * gy + cxy * gx))
            for c in range(SLOPES):
                totals[c] = [old + jnp.where(masks[c], new, 0.0) for old, new in zip(totals[c], adjoint)]

    zs = []
    for d_frac, d_gx, d_gy in totals:
        d_frac, d_gx, d_gy = (v + swap(v) for v in (d_frac, d_gx, d_gy))
        zs += [jnp.where(half, d_frac, d_gy), jnp.where(half, d_gx, 0.0)]
    upper, lower = split(jnp.concatenate(zs, axis=0) * STEEP, 2)
    spread = dot(upper, back_c[...]) + dot(lower, back_c[...])
    deep = 2 * cells_x
    own = None
    for c in range(SLOPES):
        pixels = dot(back_r2[...], jnp.concatenate(split(spread[c * deep : (c + 1) * deep], 2), axis=0))
        own = pixels * soft[c] if c == 0 else own + pixels * soft[c]

    gpad[mid_r, mid_c] = own
    halo_each(gpad, 1, "start", (True,))
    pack_strips(gpad, 1)
    halo_each(gpad, 1, "start", (False,))
    write_grad = pltpu.make_async_copy(gpad.at[mid_r, mid_c], grad_out, out_sem.at[0])
    write_grad.start()
    halo_each(gpad, 1, "wait_recv")
    unpack_strips(gpad, 1)
    writes = [write_grad]
    for i, part in enumerate(smooth(gpad, band_c, band_r, rows, cols, 2)):
        at = pl.ds(i * BAND_COLS, BAND_COLS)
        result[:, at] = part
        write = pltpu.make_async_copy(result.at[:, at], dens_out.at[:, at], out_sem.at[i + 1])
        write.start()
        writes.append(write)

    halo_each(pad, 0, "wait_send")
    halo_each(gpad, 1, "wait_send")
    for k in range(1, nz):
        cot_copy(k, True).wait_send()
    for write in writes:
        write.wait()


def on_device(density, cot, slope, layer_block, block_eps, nx, nz):
    rows, cols = density.shape
    comps, local = cot.shape[:2]
    cells_x = rows // SUB
    tall, wide = rows + 2 * RADIUS, cols + 2 * LANES
    packed = (nz, comps * (local // 2) + 1, cells_x, LANES)
    strips = (2, 2, (rows + 2 * RADIUS) * RADIUS // LANES, LANES)
    hbm = pl.BlockSpec(memory_space=pltpu.HBM)
    smem = pl.BlockSpec(memory_space=pltpu.SMEM)
    dma = pltpu.SemaphoreType.DMA
    near = len(NEAR)
    shape = jax.ShapeDtypeStruct((rows, cols), F32)
    return pl.pallas_call(
        functools.partial(kernel, nx, nz, rows, cols, local),
        out_shape=(shape, shape),
        in_specs=[smem, smem, hbm, hbm, hbm],
        out_specs=(hbm, hbm),
        scratch_shapes=[
            pltpu.VMEM((tall, wide), F32),
            pltpu.VMEM((tall, wide), F32),
            pltpu.VMEM(strips, F32),
            pltpu.VMEM(strips, F32),
            pltpu.VMEM(cot.shape, F32),
            pltpu.VMEM(block_eps.shape[::-1], F32),
            pltpu.VMEM(packed, F32),
            pltpu.VMEM(packed, F32),
            pltpu.VMEM((rows, cols), F32),
            pltpu.VMEM((SLOPES, rows, cols), F32),
            pltpu.VMEM((rows, cols), F32),
            pltpu.VMEM((BAND_COLS + 2 * LANES, BAND_COLS), BF16),
            pltpu.VMEM((rows, tall), BF16),
            pltpu.VMEM((cols, LANES), BF16),
            pltpu.VMEM((LANES, cols), BF16),
            pltpu.VMEM((2 * cells_x, 2 * rows), BF16),
            pltpu.VMEM((rows, 4 * cells_x), BF16),
            dma((3,)), dma((1 + cols // BAND_COLS,)),
            dma((2, near)), dma((2, near)), dma((nz,)), dma((nz,)),
        ],
        compiler_params=pltpu.CompilerParams(
            collective_id=0, has_side_effects=True, vmem_limit_bytes=60 * 1024 * 1024),
    )(slope, layer_block, block_eps.T, density, cot)


def solution(mesh):
    body = functools.partial(on_device, nx=mesh.shape["xy"], nz=mesh.shape["gz"])
    return jax.shard_map(
        body,
        mesh=mesh,
        in_specs=(P("xy", "gz"), P(None, "gz", "xy", None), P("gz"), P("gz"), P()),
        out_specs=(P("xy", "gz"), P("xy", "gz")),
        check_vma=False,
    )
```

```python
import functools
import math

import jax
import jax.numpy as jnp
from jax import lax
from jax.experimental import pallas as pl
from jax.experimental.pallas import tpu as pltpu
from jax.sharding import PartitionSpec as P

SUB = 8
RADIUS = 32
SLOPES = 5
LANES = 128
BAND_COLS = 256
STEEP = 32.0
MESH = pl.DeviceIdType.MESH
F32 = jnp.float32
BF16 = jnp.bfloat16
NEAR = [(dx, dz) for dx in (-1, 0, 1) for dz in (-1, 0, 1) if (dx, dz) != (0, 0)]


def split(value, terms):
    parts = []
    for _ in range(terms):
        part = value.astype(BF16)
        parts.append(part)
        value = value - part.astype(F32)
    return parts


def iota(shape, dim):
    return lax.broadcasted_iota(jnp.int32, shape, dim)


def taps(offset):
    return jnp.maximum(RADIUS + 1 - jnp.abs(offset), 0).astype(F32).astype(BF16)


def col_band():
    shape = (BAND_COLS + 2 * LANES, BAND_COLS)
    return taps(iota(shape, 0) - LANES - iota(shape, 1))


def row_band(height):
    shape = (height, height + 2 * RADIUS)
    return taps(iota(shape, 1) - RADIUS - iota(shape, 0))


def pool_values(cell, place, other):
    offset = (2 * (place % SUB) + 1 - SUB).astype(F32) / 2.0
    inside = place // SUB == cell % other
    values = jnp.where(cell < other, 1.0, offset) / float(SUB)
    return jnp.where(inside, values, 0.0).astype(BF16)


def col_pool(width):
    shape = (width, 2 * width // SUB)
    return pool_values(iota(shape, 1), iota(shape, 0), width // SUB)


def col_pool_t(width):
    shape = (2 * width // SUB, width)
    return pool_values(iota(shape, 0), iota(shape, 1), width // SUB)


def row_pool(height):
    shape = (2 * height // SUB, height)
    return pool_values(iota(shape, 0), iota(shape, 1), height // SUB)


def row_pool_t(height):
    shape = (height, 2 * height // SUB)
    return pool_values(iota(shape, 1), iota(shape, 0), height // SUB)


def dot(a, b):
    return jnp.dot(a, b, preferred_element_type=F32)


def smooth(pad, band_c, band_r, height, width, terms):
    scale = 1.0 / float((RADIUS + 1) ** 4)
    out = []
    for start in range(0, width, BAND_COLS):
        part = pad[:, start : start + BAND_COLS + 2 * LANES]
        across = sum(dot(x, band_c[...]) for x in split(part, terms))
        total = sum(dot(band_r[...], x) for x in split(across, terms))
        out.append(total * scale)
    return out


def pack_cols(block):
    groups = LANES // RADIUS
    height = block.shape[0] // groups
    lane = iota((1, LANES), 1)
    out = block[:height]
    for j in range(1, groups):
        moved = pltpu.roll(block[j * height : (j + 1) * height], j * RADIUS, 1)
        out = jnp.where(lane >= j * RADIUS, moved, out)
    return out


def unpack_strips(strips, target, rows, cols):
    groups = LANES // RADIUS
    quarter, corner = rows // groups, RADIUS // groups
    for side, column, shift in ((0, 0, LANES - RADIUS), (1, LANES + cols, 0)):
        for first, height, at in ((0, quarter, RADIUS), (quarter, corner, RADIUS + rows), (quarter + corner, corner, 0)):
            packed = strips[side, first : first + height]
            for j in range(groups):
                turn = (shift - j * RADIUS) % LANES
                moved = pltpu.roll(packed, turn, 1) if turn else packed
                target[at + j * height : at + (j + 1) * height, column : column + LANES] = moved


def finish(rows, cols, flat_hbm, strips_hbm, grad_out, dens_out, pad, strips, result, band_c, band_r, in_sem, out_sem):
    mid_c = pl.ds(LANES, cols)
    fetch_flat = pltpu.make_async_copy(flat_hbm, pad.at[:, mid_c], in_sem.at[0])
    fetch_strips = pltpu.make_async_copy(strips_hbm, strips, in_sem.at[1])
    fetch_flat.start()
    fetch_strips.start()
    band_c[...] = col_band()
    band_r[...] = row_band(rows)
    fetch_strips.wait()
    unpack_strips(strips, pad, rows, cols)
    fetch_flat.wait()
    writes = [pltpu.make_async_copy(pad.at[pl.ds(RADIUS, rows), mid_c], grad_out, out_sem.at[0])]
    writes[0].start()
    for i, part in enumerate(smooth(pad, band_c, band_r, rows, cols, 2)):
        at = pl.ds(i * BAND_COLS, BAND_COLS)
        result[:, at] = part
        write = pltpu.make_async_copy(result.at[:, at], dens_out.at[:, at], out_sem.at[i + 1])
        write.start()
        writes.append(write)
    for write in writes:
        write.wait()


def kernel(nx, nz, rows, cols, local, slope, block, eps_hbm, density_hbm, cot_hbm, flat_out, strips_out,
           pad, gpad, strip_out, strip_in, cot, eps, stage, recv, power, soft,
           band_c, band_r, pool_c, back_c, pool_r2, back_r2,
           in_sem, out_sem, halo_send, halo_recv, cot_send, cot_recv):
    x = lax.axis_index("xy")
    z = lax.axis_index("gz")
    cells_x, cells_y = rows // SUB, cols // SUB
    tall, wide = rows + 2 * RADIUS, cols + 2 * LANES
    mid_r, mid_c = pl.ds(RADIUS, rows), pl.ds(LANES, cols)
    groups = LANES // RADIUS

    fetch_density = pltpu.make_async_copy(density_hbm, pad.at[mid_r, mid_c], in_sem.at[0])
    fetch_cot = pltpu.make_async_copy(cot_hbm, cot, in_sem.at[1])
    fetch_eps = pltpu.make_async_copy(eps_hbm, eps, in_sem.at[2])
    fetch_density.start()
    fetch_eps.start()
    fetch_cot.start()

    def exists(dx, dz):
        ok = None
        for pos, delta, count in ((x, dx, nx), (z, dz, nz)):
            if delta == -1:
                here = pos > 0
            elif delta == 1:
                here = pos < count - 1
            else:
                continue
            ok = here if ok is None else jnp.logical_and(ok, here)
        return ok

    for ref in (pad, gpad):
        ref[0:RADIUS, mid_c] = jnp.zeros((RADIUS, cols), F32)
        ref[RADIUS + rows : tall, mid_c] = jnp.zeros((RADIUS, cols), F32)
    strip_in[...] = jnp.zeros(strip_in.shape, F32)

    barrier = pltpu.get_barrier_semaphore()
    far = [(dx, dz) for dx, dz in NEAR if dx != 0]
    for k in range(1, nz):
        pl.semaphore_signal(barrier, inc=1, device_id=(x, lax.rem(z + k, nz)), device_id_type=MESH)
    for dx, dz in far:
        @pl.when(exists(dx, dz))
        def _():
            pl.semaphore_signal(barrier, inc=1, device_id=(x + dx, z + dz), device_id_type=MESH)

    quarter, corner = rows // groups, RADIUS // groups
    spots = {0: (0, quarter), -1: (quarter, corner), 1: (quarter + corner, corner)}

    def pack_strips(source, phase):
        for side, start in ((0, 0), (1, cols - LANES)):
            edge = source[RADIUS : RADIUS + rows, LANES + start : 2 * LANES + start]
            if side == 1:
                edge = pltpu.roll(edge, RADIUS, 1)
            strip_out[phase, side, 0:quarter] = pack_cols(edge)
            strip_out[phase, side, quarter : quarter + corner] = pack_cols(edge[:RADIUS])
            strip_out[phase, side, quarter + corner :] = pack_cols(edge[rows - RADIUS :])

    def halo(target, phase, d):
        dx, dz = NEAR[d]
        if dz == 0:
            src = target.at[pl.ds(RADIUS if dx < 0 else rows, RADIUS), mid_c]
            dst = target.at[pl.ds(RADIUS + rows if dx < 0 else 0, RADIUS), mid_c]
        else:
            at = pl.ds(*spots[dx])
            src = strip_out.at[phase, 0 if dz < 0 else 1, at]
            dst = strip_in.at[phase, 1 if dz < 0 else 0, at]
        return pltpu.make_async_remote_copy(
            src_ref=src, dst_ref=dst, send_sem=halo_send.at[phase, d], recv_sem=halo_recv.at[phase, d],
            device_id=(x + dx, z + dz), device_id_type=MESH)

    def halo_each(target, phase, what, flat=(True, False)):
        for d, (dx, dz) in enumerate(NEAR):
            if (dz == 0) in flat:
                copy = halo(target, phase, d)
                where = exists(-dx, -dz) if what == "wait_recv" else exists(dx, dz)
                pl.when(where)(getattr(copy, what))

    fetch_density.wait()
    pack_strips(pad, 0)
    half = iota((1, LANES), 1) < cells_y
    swap = lambda v: pltpu.roll(v, cells_y, 1)
    comps = cot.shape[0]
    fetch_eps.wait()
    lines = []
    for k in range(local // 2):
        a, b = 2 * k, 2 * k + 1
        lines.append(jnp.where(half, slope[a].astype(F32), slope[b].astype(F32)))
        pair = jnp.where(half, block[a], block[b])
        for j in range(2):
            line = jnp.zeros((1, LANES), F32)
            for m in range(eps.shape[1]):
                line = jnp.where(pair == m, eps[j : j + 1, m : m + 1], line)
            lines.append(line)
    lines.append(jnp.zeros((8 - len(lines), LANES), F32))
    lines = jnp.concatenate(lines, axis=0)
    fetch_cot.wait()
    for c in range(comps):
        for k in range(local // 2):
            for h in range(nz // 2):
                a = cot[c, 2 * k, :, h * LANES : (h + 1) * LANES]
                b = cot[c, 2 * k + 1, :, h * LANES : (h + 1) * LANES]
                stage[2 * h, pl.ds((c * (local // 2) + k) * cells_x, cells_x)] = jnp.where(half, a, swap(b))
                stage[2 * h + 1, pl.ds((c * (local // 2) + k) * cells_x, cells_x)] = jnp.where(half, swap(a), b)
    for g in range(nz):
        stage[g, pl.ds(comps * (local // 2) * cells_x, 8)] = lines

    def cot_copy(k, outgoing):
        peer = lax.rem(z + k, nz)
        slot = z if outgoing else peer
        return pltpu.make_async_remote_copy(
            src_ref=stage.at[peer], dst_ref=recv.at[slot], send_sem=cot_send.at[k], recv_sem=cot_recv.at[slot],
            device_id=(x, peer), device_id_type=MESH)

    pl.semaphore_wait(barrier, nz - 1 + sum(jnp.where(exists(dx, dz), 1, 0) for dx, dz in far))
    halo_each(pad, 0, "start")

    for k in range(1, nz):
        cot_copy(k, True).start()

    band_c[...] = col_band()
    band_r[...] = row_band(rows)
    pool_c[...] = col_pool(cols)
    back_c[...] = col_pool_t(cols)
    pool_r = row_pool(rows)
    pool_r2[...] = jnp.concatenate([pool_r, pool_r], axis=1)
    back_r = row_pool_t(rows)
    back_r2[...] = jnp.concatenate([back_r, back_r], axis=1)

    halo_each(pad, 0, "wait_recv")
    unpack_strips(strip_in.at[0], pad, rows, cols)
    for i, part in enumerate(smooth(pad, band_c, band_r, rows, cols, 3)):
        power[:, i * BAND_COLS : (i + 1) * BAND_COLS] = jnp.exp(STEEP * (0.5 - part))

    moments = []
    for c in range(SLOPES):
        fill = 1.0 / (1.0 + power[...] * math.exp(STEEP * 0.02 * (c - 2)))
        soft[c] = fill * (1.0 - fill)
        upper, lower = split(fill, 2)
        pooled = dot(upper, pool_c[...]) + dot(lower, pool_c[...])
        cell = dot(pool_r2[...], jnp.concatenate(split(pooled, 2), axis=0))
        top, low = cell[:cells_x], cell[cells_x:]
        turned = swap(top)
        moments.append((jnp.where(half, top, turned), jnp.where(half, low, swap(low)), jnp.where(half, turned, top)))

    totals = [[jnp.zeros((cells_x, LANES), F32)] * 3 for _ in range(SLOPES)]
    for g in range(nz):
        slot = lax.rem(z + g, nz)
        if g:
            cot_copy(g, False).wait_recv()
        held = recv if g else stage
        for k in range(local // 2):
            at = comps * (local // 2) * cells_x + 3 * k
            kind, e1, e2 = (held[slot, at + j : at + j + 1, :] for j in range(3))
            cxx, cyy, czz, cxy, cxz, cyz = (held[slot, pl.ds((c * (local // 2) + k) * cells_x, cells_x)] for c in range(comps))
            masks = [jnp.broadcast_to(kind == float(c), (cells_x, LANES)) for c in range(SLOPES)]
            frac, gx, gy = moments[0]
            for c in range(1, SLOPES):
                frac, gx, gy = (jnp.where(masks[c], new, old) for new, old in zip(moments[c], (frac, gx, gy)))
            cz = 0.2 * (1.0 + kind)
            step = e1 - e2
            inv2 = 1.0 / e2
            inv_step = 1.0 / e1 - inv2
            norm = 1.0 / (gx * gx + gy * gy + cz * cz)
            mean = e2 + frac * step
            harm = 1.0 / (inv2 + frac * inv_step)
            weight = (harm - mean) * norm
            px = cxx * gx + cxy * gy + cxz * cz
            py = cyy * gy + cyz * cz
            quad = (gx * px + gy * py + cz * cz * czz) * norm
            adjoint = ((cxx + cyy + czz - quad) * step - quad * harm * harm * inv_step,
                       weight * (px + (cxx - 2.0 * quad) * gx),
                       weight * (py + (cyy - 2.0 * quad) * gy + cxy * gx))
            for c in range(SLOPES):
                totals[c] = [old + jnp.where(masks[c], new, 0.0) for old, new in zip(totals[c], adjoint)]

    zs = []
    for d_frac, d_gx, d_gy in totals:
        d_frac, d_gx, d_gy = (v + swap(v) for v in (d_frac, d_gx, d_gy))
        zs += [jnp.where(half, d_frac, d_gy), jnp.where(half, d_gx, 0.0)]
    upper, lower = split(jnp.concatenate(zs, axis=0) * STEEP, 2)
    spread = dot(upper, back_c[...]) + dot(lower, back_c[...])
    deep = 2 * cells_x
    own = None
    for c in range(SLOPES):
        pixels = dot(back_r2[...], jnp.concatenate(split(spread[c * deep : (c + 1) * deep], 2), axis=0))
        own = pixels * soft[c] if c == 0 else own + pixels * soft[c]

    gpad[mid_r, mid_c] = own
    halo_each(gpad, 1, "start", (True,))
    pack_strips(gpad, 1)
    halo_each(gpad, 1, "start", (False,))
    writes = [pltpu.make_async_copy(gpad.at[mid_r, mid_c], flat_out.at[mid_r], out_sem.at[0])]
    writes[0].start()
    halo_each(gpad, 1, "wait_recv")
    top, bottom = pl.ds(0, RADIUS), pl.ds(RADIUS + rows, RADIUS)
    writes += [pltpu.make_async_copy(gpad.at[top, mid_c], flat_out.at[top], out_sem.at[1]),
               pltpu.make_async_copy(gpad.at[bottom, mid_c], flat_out.at[bottom], out_sem.at[2]),
               pltpu.make_async_copy(strip_in.at[1], strips_out, out_sem.at[3])]
    for write in writes[1:]:
        write.start()

    halo_each(pad, 0, "wait_send")
    halo_each(gpad, 1, "wait_send")
    for k in range(1, nz):
        cot_copy(k, True).wait_send()
    for write in writes:
        write.wait()


def on_device(density, cot, slope, layer_block, block_eps, nx, nz):
    rows, cols = density.shape
    comps, local = cot.shape[:2]
    cells_x = rows // SUB
    tall, wide = rows + 2 * RADIUS, cols + 2 * LANES
    packed = (nz, comps * (local // 2) * cells_x + 8, LANES)
    strips = (2, 2, (rows + 2 * RADIUS) * RADIUS // LANES, LANES)
    hbm = pl.BlockSpec(memory_space=pltpu.HBM)
    smem = pl.BlockSpec(memory_space=pltpu.SMEM)
    dma = pltpu.SemaphoreType.DMA
    near = len(NEAR)
    shape = jax.ShapeDtypeStruct((rows, cols), F32)
    flat, packed_strips = pl.pallas_call(
        functools.partial(kernel, nx, nz, rows, cols, local),
        out_shape=(jax.ShapeDtypeStruct((tall, cols), F32), jax.ShapeDtypeStruct(strips[1:], F32)),
        in_specs=[smem, smem, hbm, hbm, hbm],
        out_specs=(hbm, hbm),
        scratch_shapes=[
            pltpu.VMEM((tall, wide), F32),
            pltpu.VMEM((tall, wide), F32),
            pltpu.VMEM(strips, F32),
            pltpu.VMEM(strips, F32),
            pltpu.VMEM(cot.shape, F32),
            pltpu.VMEM(block_eps.shape[::-1], F32),
            pltpu.VMEM(packed, F32),
            pltpu.VMEM(packed, F32),
            pltpu.VMEM((rows, cols), F32),
            pltpu.VMEM((SLOPES, rows, cols), F32),
            pltpu.VMEM((BAND_COLS + 2 * LANES, BAND_COLS), BF16),
            pltpu.VMEM((rows, tall), BF16),
            pltpu.VMEM((cols, LANES), BF16),
            pltpu.VMEM((LANES, cols), BF16),
            pltpu.VMEM((2 * cells_x, 2 * rows), BF16),
            pltpu.VMEM((rows, 4 * cells_x), BF16),
            dma((3,)), dma((4,)),
            dma((2, near)), dma((2, near)), dma((nz,)), dma((nz,)),
        ],
        compiler_params=pltpu.CompilerParams(
            collective_id=0, has_side_effects=True, vmem_limit_bytes=60 * 1024 * 1024),
    )(slope, layer_block, block_eps.T, density, cot)
    return pl.pallas_call(
        functools.partial(finish, rows, cols),
        out_shape=(shape, shape),
        in_specs=[hbm, hbm],
        out_specs=(hbm, hbm),
        scratch_shapes=[
            pltpu.VMEM((tall, wide), F32),
            pltpu.VMEM(strips[1:], F32),
            pltpu.VMEM((rows, cols), F32),
            pltpu.VMEM((BAND_COLS + 2 * LANES, BAND_COLS), BF16),
            pltpu.VMEM((rows, tall), BF16),
            dma((2,)), dma((1 + cols // BAND_COLS,)),
        ],
        compiler_params=pltpu.CompilerParams(vmem_limit_bytes=60 * 1024 * 1024),
    )(flat, packed_strips)


def solution(mesh):
    body = functools.partial(on_device, nx=mesh.shape["xy"], nz=mesh.shape["gz"])
    return jax.shard_map(
        body,
        mesh=mesh,
        in_specs=(P("xy", "gz"), P(None, "gz", "xy", None), P("gz"), P("gz"), P()),
        out_specs=(P("xy", "gz"), P("xy", "gz")),
        check_vma=False,
    )
```

```python
import functools
import math

import jax
import jax.numpy as jnp
from jax import lax
from jax.experimental import pallas as pl
from jax.experimental.pallas import tpu as pltpu
from jax.sharding import PartitionSpec as P

SUB = 8
RADIUS = 32
SLOPES = 5
LANES = 128
BAND_COLS = 256
STEEP = 32.0
MESH = pl.DeviceIdType.MESH
F32 = jnp.float32
BF16 = jnp.bfloat16
NEAR = [(dx, dz) for dx in (-1, 0, 1) for dz in (-1, 0, 1) if (dx, dz) != (0, 0)]


def split(value, terms):
    parts = []
    for _ in range(terms):
        part = value.astype(BF16)
        parts.append(part)
        value = value - part.astype(F32)
    return parts


def iota(shape, dim):
    return lax.broadcasted_iota(jnp.int32, shape, dim)


def taps(offset):
    return jnp.maximum(RADIUS + 1 - jnp.abs(offset), 0).astype(F32).astype(BF16)


def col_band():
    shape = (BAND_COLS + 2 * LANES, BAND_COLS)
    return taps(iota(shape, 0) - LANES - iota(shape, 1))


def row_band(height):
    shape = (height, height + 2 * RADIUS)
    return taps(iota(shape, 1) - RADIUS - iota(shape, 0))


def pool_values(cell, place, other):
    offset = (2 * (place % SUB) + 1 - SUB).astype(F32) / 2.0
    inside = place // SUB == cell % other
    values = jnp.where(cell < other, 1.0, offset) / float(SUB)
    return jnp.where(inside, values, 0.0).astype(BF16)


def col_pool(width):
    shape = (width, 2 * width // SUB)
    return pool_values(iota(shape, 1), iota(shape, 0), width // SUB)


def col_pool_t(width):
    shape = (2 * width // SUB, width)
    return pool_values(iota(shape, 0), iota(shape, 1), width // SUB)


def row_pool(height):
    shape = (2 * height // SUB, height)
    return pool_values(iota(shape, 0), iota(shape, 1), height // SUB)


def row_pool_t(height):
    shape = (height, 2 * height // SUB)
    return pool_values(iota(shape, 1), iota(shape, 0), height // SUB)


def dot(a, b):
    return jnp.dot(a, b, preferred_element_type=F32)


def smooth(pad, band_c, band_r, height, width, terms):
    scale = 1.0 / float((RADIUS + 1) ** 4)
    out = []
    for start in range(0, width, BAND_COLS):
        part = pad[:, start : start + BAND_COLS + 2 * LANES]
        across = sum(dot(x, band_c[...]) for x in split(part, terms))
        total = sum(dot(band_r[...], x) for x in split(across, terms))
        out.append(total * scale)
    return out


def pack_cols(block):
    groups = LANES // RADIUS
    height = block.shape[0] // groups
    lane = iota((1, LANES), 1)
    out = block[:height]
    for j in range(1, groups):
        moved = pltpu.roll(block[j * height : (j + 1) * height], j * RADIUS, 1)
        out = jnp.where(lane >= j * RADIUS, moved, out)
    return out


def unpack_strips(strips, target, rows, cols):
    groups = LANES // RADIUS
    quarter, corner = rows // groups, RADIUS // groups
    for side, column, shift in ((0, 0, LANES - RADIUS), (1, LANES + cols, 0)):
        for first, height, at in ((0, quarter, RADIUS), (quarter, corner, RADIUS + rows), (quarter + corner, corner, 0)):
            packed = strips[side, first : first + height]
            for j in range(groups):
                turn = (shift - j * RADIUS) % LANES
                moved = pltpu.roll(packed, turn, 1) if turn else packed
                target[at + j * height : at + (j + 1) * height, column : column + LANES] = moved


def finish(rows, cols, flat_hbm, strips_hbm, grad_out, dens_out, pad, strips, result, band_c, band_r, in_sem, out_sem):
    mid_c = pl.ds(LANES, cols)
    fetch_flat = pltpu.make_async_copy(flat_hbm, pad.at[:, mid_c], in_sem.at[0])
    fetch_strips = pltpu.make_async_copy(strips_hbm, strips, in_sem.at[1])
    fetch_flat.start()
    fetch_strips.start()
    band_c[...] = col_band()
    band_r[...] = row_band(rows)
    fetch_strips.wait()
    unpack_strips(strips, pad, rows, cols)
    fetch_flat.wait()
    writes = [pltpu.make_async_copy(pad.at[pl.ds(RADIUS, rows), mid_c], grad_out, out_sem.at[0])]
    writes[0].start()
    for i, part in enumerate(smooth(pad, band_c, band_r, rows, cols, 2)):
        at = pl.ds(i * BAND_COLS, BAND_COLS)
        result[:, at] = part
        write = pltpu.make_async_copy(result.at[:, at], dens_out.at[:, at], out_sem.at[i + 1])
        write.start()
        writes.append(write)
    for write in writes:
        write.wait()


def kernel(nx, nz, rows, cols, local, slope, block, eps_hbm, density_hbm, cot_hbm, flat_out, strips_out,
           pad, gpad, strip_out, strip_in, cot, eps, stage, recv, power, soft,
           band_c, band_r, pool_c, back_c, pool_r2, back_r2,
           in_sem, out_sem, halo_send, halo_recv, cot_send, cot_recv):
    x = lax.axis_index("xy")
    z = lax.axis_index("gz")
    cells_x, cells_y = rows // SUB, cols // SUB
    tall, wide = rows + 2 * RADIUS, cols + 2 * LANES
    mid_r, mid_c = pl.ds(RADIUS, rows), pl.ds(LANES, cols)
    groups = LANES // RADIUS

    fetch_density = pltpu.make_async_copy(density_hbm, pad.at[mid_r, mid_c], in_sem.at[0])
    fetch_cot = pltpu.make_async_copy(cot_hbm, cot, in_sem.at[1])
    fetch_eps = pltpu.make_async_copy(eps_hbm, eps, in_sem.at[2])
    fetch_density.start()
    fetch_eps.start()
    fetch_cot.start()

    def exists(dx, dz):
        ok = None
        for pos, delta, count in ((x, dx, nx), (z, dz, nz)):
            if delta == -1:
                here = pos > 0
            elif delta == 1:
                here = pos < count - 1
            else:
                continue
            ok = here if ok is None else jnp.logical_and(ok, here)
        return ok

    for ref in (pad, gpad):
        ref[0:RADIUS, mid_c] = jnp.zeros((RADIUS, cols), F32)
        ref[RADIUS + rows : tall, mid_c] = jnp.zeros((RADIUS, cols), F32)
    strip_in[...] = jnp.zeros(strip_in.shape, F32)

    barrier = pltpu.get_barrier_semaphore()
    far = [(dx, dz) for dx, dz in NEAR if dx != 0]
    for k in range(1, nz):
        pl.semaphore_signal(barrier, inc=1, device_id=(x, lax.rem(z + k, nz)), device_id_type=MESH)
    for dx, dz in far:
        @pl.when(exists(dx, dz))
        def _():
            pl.semaphore_signal(barrier, inc=1, device_id=(x + dx, z + dz), device_id_type=MESH)

    quarter, corner = rows // groups, RADIUS // groups
    spots = {0: (0, quarter), -1: (quarter, corner), 1: (quarter + corner, corner)}

    def pack_strips(source, phase):
        for side, start in ((0, 0), (1, cols - LANES)):
            edge = source[RADIUS : RADIUS + rows, LANES + start : 2 * LANES + start]
            if side == 1:
                edge = pltpu.roll(edge, RADIUS, 1)
            strip_out[phase, side, 0:quarter] = pack_cols(edge)
            strip_out[phase, side, quarter : quarter + corner] = pack_cols(edge[:RADIUS])
            strip_out[phase, side, quarter + corner :] = pack_cols(edge[rows - RADIUS :])

    def halo(target, phase, d):
        dx, dz = NEAR[d]
        if dz == 0:
            src = target.at[pl.ds(RADIUS if dx < 0 else rows, RADIUS), mid_c]
            dst = target.at[pl.ds(RADIUS + rows if dx < 0 else 0, RADIUS), mid_c]
        else:
            at = pl.ds(*spots[dx])
            src = strip_out.at[phase, 0 if dz < 0 else 1, at]
            dst = strip_in.at[phase, 1 if dz < 0 else 0, at]
        return pltpu.make_async_remote_copy(
            src_ref=src, dst_ref=dst, send_sem=halo_send.at[phase, d], recv_sem=halo_recv.at[phase, d],
            device_id=(x + dx, z + dz), device_id_type=MESH)

    def halo_each(target, phase, what, flat=(True, False)):
        for d, (dx, dz) in enumerate(NEAR):
            if (dz == 0) in flat:
                copy = halo(target, phase, d)
                where = exists(-dx, -dz) if what == "wait_recv" else exists(dx, dz)
                pl.when(where)(getattr(copy, what))

    fetch_density.wait()
    pack_strips(pad, 0)
    half = iota((1, LANES), 1) < cells_y
    swap = lambda v: pltpu.roll(v, cells_y, 1)
    comps = cot.shape[0]
    fetch_eps.wait()
    lines = []
    for k in range(local // 2):
        a, b = 2 * k, 2 * k + 1
        lines.append(jnp.where(half, slope[a].astype(F32), slope[b].astype(F32)))
        pair = jnp.where(half, block[a], block[b])
        for j in range(2):
            line = jnp.zeros((1, LANES), F32)
            for m in range(eps.shape[1]):
                line = jnp.where(pair == m, eps[j : j + 1, m : m + 1], line)
            lines.append(line)
    lines.append(jnp.zeros((8 - len(lines), LANES), F32))
    lines = jnp.concatenate(lines, axis=0)
    fetch_cot.wait()
    for c in range(comps):
        for k in range(local // 2):
            for h in range(nz // 2):
                a = cot[c, 2 * k, :, h * LANES : (h + 1) * LANES]
                b = cot[c, 2 * k + 1, :, h * LANES : (h + 1) * LANES]
                stage[2 * h, pl.ds(8 + (k * comps + c) * cells_x, cells_x)] = jnp.where(half, a, swap(b))
                stage[2 * h + 1, pl.ds(8 + (k * comps + c) * cells_x, cells_x)] = jnp.where(half, swap(a), b)
    for g in range(nz):
        stage[g, pl.ds(0, 8)] = lines

    def cot_copy(part, k, outgoing):
        at = pl.ds(8 + part * comps * cells_x if part else 0, comps * cells_x + (0 if part else 8))
        peer = lax.rem(z + k, nz)
        slot = z if outgoing else peer
        return pltpu.make_async_remote_copy(
            src_ref=stage.at[peer, at], dst_ref=recv.at[slot, at],
            send_sem=cot_send.at[part, k], recv_sem=cot_recv.at[part, slot],
            device_id=(x, peer), device_id_type=MESH)

    pl.semaphore_wait(barrier, nz - 1 + sum(jnp.where(exists(dx, dz), 1, 0) for dx, dz in far))
    halo_each(pad, 0, "start")

    for part in range(local // 2):
        for k in range(1, nz):
            cot_copy(part, k, True).start()

    band_c[...] = col_band()
    band_r[...] = row_band(rows)
    pool_c[...] = col_pool(cols)
    back_c[...] = col_pool_t(cols)
    pool_r = row_pool(rows)
    pool_r2[...] = jnp.concatenate([pool_r, pool_r], axis=1)
    back_r = row_pool_t(rows)
    back_r2[...] = jnp.concatenate([back_r, back_r], axis=1)

    halo_each(pad, 0, "wait_recv")
    unpack_strips(strip_in.at[0], pad, rows, cols)
    for i, part in enumerate(smooth(pad, band_c, band_r, rows, cols, 3)):
        power[:, i * BAND_COLS : (i + 1) * BAND_COLS] = jnp.exp(STEEP * (0.5 - part))

    moments = []
    for c in range(SLOPES):
        fill = 1.0 / (1.0 + power[...] * math.exp(STEEP * 0.02 * (c - 2)))
        soft[c] = fill * (1.0 - fill)
        upper, lower = split(fill, 2)
        pooled = dot(upper, pool_c[...]) + dot(lower, pool_c[...])
        cell = dot(pool_r2[...], jnp.concatenate(split(pooled, 2), axis=0))
        top, low = cell[:cells_x], cell[cells_x:]
        turned = swap(top)
        moments.append((jnp.where(half, top, turned), jnp.where(half, low, swap(low)), jnp.where(half, turned, top)))

    totals = [[jnp.zeros((cells_x, LANES), F32)] * 3 for _ in range(SLOPES)]
    for k in range(local // 2):
        for g in range(nz):
            slot = lax.rem(z + g, nz)
            if g:
                cot_copy(k, g, False).wait_recv()
            held = recv if g else stage
            at = 3 * k
            kind, e1, e2 = (held[slot, at + j : at + j + 1, :] for j in range(3))
            cxx, cyy, czz, cxy, cxz, cyz = (held[slot, pl.ds(8 + (k * comps + c) * cells_x, cells_x)] for c in range(comps))
            masks = [jnp.broadcast_to(kind == float(c), (cells_x, LANES)) for c in range(SLOPES)]
            frac, gx, gy = moments[0]
            for c in range(1, SLOPES):
                frac, gx, gy = (jnp.where(masks[c], new, old) for new, old in zip(moments[c], (frac, gx, gy)))
            cz = 0.2 * (1.0 + kind)
            step = e1 - e2
            inv2 = 1.0 / e2
            inv_step = 1.0 / e1 - inv2
            norm = 1.0 / (gx * gx + gy * gy + cz * cz)
            mean = e2 + frac * step
            harm = 1.0 / (inv2 + frac * inv_step)
            weight = (harm - mean) * norm
            px = cxx * gx + cxy * gy + cxz * cz
            py = cyy * gy + cyz * cz
            quad = (gx * px + gy * py + cz * cz * czz) * norm
            adjoint = ((cxx + cyy + czz - quad) * step - quad * harm * harm * inv_step,
                       weight * (px + (cxx - 2.0 * quad) * gx),
                       weight * (py + (cyy - 2.0 * quad) * gy + cxy * gx))
            for c in range(SLOPES):
                totals[c] = [old + jnp.where(masks[c], new, 0.0) for old, new in zip(totals[c], adjoint)]

    zs = []
    for d_frac, d_gx, d_gy in totals:
        d_frac, d_gx, d_gy = (v + swap(v) for v in (d_frac, d_gx, d_gy))
        zs += [jnp.where(half, d_frac, d_gy), jnp.where(half, d_gx, 0.0)]
    upper, lower = split(jnp.concatenate(zs, axis=0) * STEEP, 2)
    spread = dot(upper, back_c[...]) + dot(lower, back_c[...])
    deep = 2 * cells_x
    own = None
    for c in range(SLOPES):
        pixels = dot(back_r2[...], jnp.concatenate(split(spread[c * deep : (c + 1) * deep], 2), axis=0))
        own = pixels * soft[c] if c == 0 else own + pixels * soft[c]

    gpad[mid_r, mid_c] = own
    halo_each(gpad, 1, "start", (True,))
    pack_strips(gpad, 1)
    halo_each(gpad, 1, "start", (False,))
    writes = [pltpu.make_async_copy(gpad.at[mid_r, mid_c], flat_out.at[mid_r], out_sem.at[0])]
    writes[0].start()
    halo_each(gpad, 1, "wait_recv")
    top, bottom = pl.ds(0, RADIUS), pl.ds(RADIUS + rows, RADIUS)
    writes += [pltpu.make_async_copy(gpad.at[top, mid_c], flat_out.at[top], out_sem.at[1]),
               pltpu.make_async_copy(gpad.at[bottom, mid_c], flat_out.at[bottom], out_sem.at[2]),
               pltpu.make_async_copy(strip_in.at[1], strips_out, out_sem.at[3])]
    for write in writes[1:]:
        write.start()

    halo_each(pad, 0, "wait_send")
    halo_each(gpad, 1, "wait_send")
    for k in range(1, nz):
        for part in range(local // 2):
            cot_copy(part, k, True).wait_send()
    for write in writes:
        write.wait()


def on_device(density, cot, slope, layer_block, block_eps, nx, nz):
    rows, cols = density.shape
    comps, local = cot.shape[:2]
    cells_x = rows // SUB
    tall, wide = rows + 2 * RADIUS, cols + 2 * LANES
    packed = (nz, comps * (local // 2) * cells_x + 8, LANES)
    strips = (2, 2, (rows + 2 * RADIUS) * RADIUS // LANES, LANES)
    hbm = pl.BlockSpec(memory_space=pltpu.HBM)
    smem = pl.BlockSpec(memory_space=pltpu.SMEM)
    dma = pltpu.SemaphoreType.DMA
    near = len(NEAR)
    shape = jax.ShapeDtypeStruct((rows, cols), F32)
    flat, packed_strips = pl.pallas_call(
        functools.partial(kernel, nx, nz, rows, cols, local),
        out_shape=(jax.ShapeDtypeStruct((tall, cols), F32), jax.ShapeDtypeStruct(strips[1:], F32)),
        in_specs=[smem, smem, hbm, hbm, hbm],
        out_specs=(hbm, hbm),
        scratch_shapes=[
            pltpu.VMEM((tall, wide), F32),
            pltpu.VMEM((tall, wide), F32),
            pltpu.VMEM(strips, F32),
            pltpu.VMEM(strips, F32),
            pltpu.VMEM(cot.shape, F32),
            pltpu.VMEM(block_eps.shape[::-1], F32),
            pltpu.VMEM(packed, F32),
            pltpu.VMEM(packed, F32),
            pltpu.VMEM((rows, cols), F32),
            pltpu.VMEM((SLOPES, rows, cols), F32),
            pltpu.VMEM((BAND_COLS + 2 * LANES, BAND_COLS), BF16),
            pltpu.VMEM((rows, tall), BF16),
            pltpu.VMEM((cols, LANES), BF16),
            pltpu.VMEM((LANES, cols), BF16),
            pltpu.VMEM((2 * cells_x, 2 * rows), BF16),
            pltpu.VMEM((rows, 4 * cells_x), BF16),
            dma((3,)), dma((4,)),
            dma((2, near)), dma((2, near)), dma((local // 2, nz)), dma((local // 2, nz)),
        ],
        compiler_params=pltpu.CompilerParams(
            collective_id=0, has_side_effects=True, vmem_limit_bytes=60 * 1024 * 1024),
    )(slope, layer_block, block_eps.T, density, cot)
    return pl.pallas_call(
        functools.partial(finish, rows, cols),
        out_shape=(shape, shape),
        in_specs=[hbm, hbm],
        out_specs=(hbm, hbm),
        scratch_shapes=[
            pltpu.VMEM((tall, wide), F32),
            pltpu.VMEM(strips[1:], F32),
            pltpu.VMEM((rows, cols), F32),
            pltpu.VMEM((BAND_COLS + 2 * LANES, BAND_COLS), BF16),
            pltpu.VMEM((rows, tall), BF16),
            dma((2,)), dma((1 + cols // BAND_COLS,)),
        ],
        compiler_params=pltpu.CompilerParams(vmem_limit_bytes=60 * 1024 * 1024),
    )(flat, packed_strips)


def solution(mesh):
    body = functools.partial(on_device, nx=mesh.shape["xy"], nz=mesh.shape["gz"])
    return jax.shard_map(
        body,
        mesh=mesh,
        in_specs=(P("xy", "gz"), P(None, "gz", "xy", None), P("gz"), P("gz"), P()),
        out_specs=(P("xy", "gz"), P("xy", "gz")),
        check_vma=False,
    )
```
